32 devices in a mesh: parts: 2 (over y), vocab: 4 (over z), docs: 4 (over x, core).
Axes of the slice: x: 2, y: 2, z: 4, core: 2. Of those that a mesh axis runs over, the one named last changes fastest.
Arguments:
- lambda_topics: float32 [2048, 4096], P('docs', 'vocab'), may hold values from 0.025 to 120, as said below
- gamma_start: float32 [2048, 2048], P(('parts', 'docs')), parts along dimension 0, may hold values from 0.5 to 2
- tile_counts: int32 [8, 4, 16, 128, 128], P(('parts', 'docs'), 'vocab'), parts along dimension 0, may hold values from 0 to 12, as said below
- tile_place: int32 [8, 4, 16, 2], P(('parts', 'docs'), 'vocab'), parts along dimension 0, may hold values from 0 to 7, as said below
- tile_live: int32 [8, 4], P(('parts', 'docs'), 'vocab'), parts along dimension 0, may hold values from 1 to 16, as said below
Outputs:
- gamma: float32 [2048, 2048], P(('parts', 'docs', 'vocab')), parts along dimension 0
- lambda_new: float32 [4096, 4096], P(('parts', 'docs'), 'vocab'), parts along dimension 0
The draws below stay inside these ranges and needn't reach their ends.
There are 2 independent parts, one for each index of `parts`. The reference program is written for one: setup_inputs(seed, part) draws one part's arguments, and reference() takes and returns one part's arrays. A program takes and returns all parts, laid end to end along the dimension named above; an argument that names none is the same for every part. Nothing has to cross between parts.
Inputs may be any that keep to these rules, and one draw needn't show every extreme that they name: `lambda_topics`: Positive. `tile_counts`: slots at or past the group's and shard's live count hold only zeros. `tile_place`: the 16 slots of each group and shard name every pair of doc block and word block of that group's documents and that shard's words once. `tile_live`: some group and shard has all 16 slots live.
All inputs are finite; a program needn't handle non-finite values.
Results may differ from the reference program's by a relative error of at most 0.02.
Values may be sent and summed in bfloat16 or wider, within the bound.
A program may use at most 128 MiB of HBM per device.

```python
import math
import jax
import jax.numpy as jnp
from jax import lax

K = 2048
TILE = 128
ITERS = 3
DOCS_DEV = 256
WORDS_DEV = 1024
SLOTS = 16
DOC_GROUPS = 4
VOCAB_SHARDS = 4
DOCS = 1024
VOCAB = 4096


def tile_layout(key):
    devices = DOC_GROUPS * VOCAB_SHARDS
    keys = jax.random.split(key, 5)
    orders = jax.vmap(lambda sub: jax.random.permutation(sub, SLOTS))(jax.random.split(keys[0], devices))
    live = jax.random.randint(keys[1], (devices,), 1, SLOTS + 1)
    fullest = jax.random.randint(keys[2], (), 0, devices)
    live = jnp.where(jnp.arange(devices) == fullest, SLOTS, live).astype(jnp.int32)
    blocks = WORDS_DEV // TILE
    place = jnp.stack([orders // blocks, orders % blocks], -1).astype(jnp.int32)
    chance = jax.random.randint(keys[3], (devices, SLOTS, TILE, TILE), 0, 10)
    values = jax.random.randint(keys[4], (devices, SLOTS, TILE, TILE), 1, 13)
    used = (jnp.arange(SLOTS)[None, :] < live[:, None]).astype(jnp.int32)
    counts = jnp.where(chance < 4, values, 0) * used[:, :, None, None]
    counts = counts.astype(jnp.int32).reshape(DOC_GROUPS, VOCAB_SHARDS, SLOTS, TILE, TILE)
    place = place.reshape(DOC_GROUPS, VOCAB_SHARDS, SLOTS, 2)
    live = live.reshape(DOC_GROUPS, VOCAB_SHARDS)
    return (counts, place, live)


def draw_tile_counts(key, part):
    return tile_layout(key)[0]


def draw_tile_place(key, part):
    return tile_layout(key)[1]


def draw_tile_live(key, part):
    return tile_layout(key)[2]


def draw_lambda_topics(key, part):
    key = jax.random.fold_in(key, 11)
    first = jax.random.fold_in(key, 0)
    third = jax.random.fold_in(key, 2)
    fourth = jax.random.fold_in(key, 3)
    base = jnp.exp(jax.random.uniform(first, (K, VOCAB), jnp.float32, math.log(0.1), math.log(10.0)))
    steep = jax.random.uniform(third, (K, 1), jnp.float32, math.log(3.0), math.log(9.0))
    sign = jnp.where(jax.random.randint(fourth, (K, 1), 0, 2) == 0, -1.0, 1.0).astype(jnp.float32)
    place = jnp.arange(VOCAB, dtype=jnp.float32)[None, :] / (VOCAB - 1) - 0.5
    ramp = jnp.exp(sign * steep * place)
    return (base * ramp).astype(jnp.float32)


def levels(rng, dims, cuts, least, top_value):
    factor_of, own = 1.0, jax.random.fold_in(rng, 6)
    for dim, blocks in cuts:
        steps = jnp.exp(jax.random.uniform(jax.random.fold_in(own, dim), (blocks,), jnp.float32, least / len(cuts), top_value / len(cuts)))
        factor_of = factor_of * jnp.repeat(steps, dims[dim] // blocks).reshape([-1 if axis == dim else 1 for axis in range(len(dims))])
    return factor_of


def setup_inputs(seed: int = 0, part: int = 0) -> dict:
    key_of = jax.random.split(jax.random.key(seed), 6)
    own_keys = jax.random.split(jax.random.fold_in(key_of[5], part), 6)
    lambda_topics = draw_lambda_topics(jax.random.fold_in(key_of[5], 71), part)
    gamma_start = jnp.clip(0.5 + 1.5 * jax.random.uniform(own_keys[1], (DOCS, K), jnp.float32) ** levels(own_keys[1], (DOCS, K), ((0, 4),), -0.2, 0.2), 0.5, 2.0)
    tile_counts = draw_tile_counts(jax.random.fold_in(jax.random.fold_in(key_of[5], part), 71), part)
    tile_place = draw_tile_place(jax.random.fold_in(jax.random.fold_in(key_of[5], part), 71), part)
    tile_live = draw_tile_live(jax.random.fold_in(jax.random.fold_in(key_of[5], part), 71), part)
    return dict(lambda_topics=lambda_topics, gamma_start=gamma_start, tile_counts=tile_counts, tile_place=tile_place, tile_live=tile_live)


alpha_prior = 0.05
eta_prior = 0.01
step_weight = 0.5
corpus_scale = 4.0


def expected_theta(gamma):
    spread = lax.digamma(gamma) - lax.digamma(jnp.sum(gamma, 1, keepdims=True))
    return jnp.exp(spread).astype(jnp.bfloat16)


def reference(lambda_topics, gamma_start, tile_counts, tile_place, tile_live):
    rowsum = jnp.sum(lambda_topics, 1, keepdims=True)
    exp_beta = jnp.exp(lax.digamma(lambda_topics) - lax.digamma(rowsum)).astype(jnp.bfloat16)
    groups = tile_live.shape[0]
    shards = tile_live.shape[1]

    def ratio_of(exp_theta, group, shard, position):
        row_start = (group * DOCS_DEV + tile_place[group, shard, position, 0] * TILE).astype(jnp.int32)
        col_start = (shard * WORDS_DEV + tile_place[group, shard, position, 1] * TILE).astype(jnp.int32)
        theta_block = lax.dynamic_slice_in_dim(exp_theta, row_start, TILE, 0)
        beta_block = lax.dynamic_slice_in_dim(exp_beta, col_start, TILE, 1)
        norm = jnp.dot(theta_block, beta_block, preferred_element_type=jnp.float32)
        weights = tile_counts[group, shard, position].astype(jnp.float32)
        ratio = (weights / norm).astype(jnp.bfloat16)
        return row_start, col_start, theta_block, beta_block, ratio

    def over_shards(group, handler, carry):
        def per_shard(shard, inner):
            return lax.fori_loop(0, tile_live[group, shard], lambda position, acc: handler(group, shard, position, acc), inner)
        return lax.fori_loop(0, shards, per_shard, carry)

    exp_theta = expected_theta(gamma_start)
    gamma = gamma_start
    for step in range(ITERS):
        def add_topics(group, shard, position, total):
            row_start, col_start, theta_block, beta_block, ratio = ratio_of(exp_theta, group, shard, position)
            part = jnp.dot(ratio, beta_block.T, preferred_element_type=jnp.float32)
            current = lax.dynamic_slice_in_dim(total, row_start, TILE, 0)
            return lax.dynamic_update_slice_in_dim(total, current + part, row_start, 0)

        total = lax.fori_loop(0, groups, lambda group, acc: over_shards(group, add_topics, acc),
                              jnp.zeros((groups * DOCS_DEV, K), jnp.float32))
        gamma = alpha_prior + exp_theta.astype(jnp.float32) * total
        exp_theta = expected_theta(gamma)

    def add_words(group, shard, position, partial_value):
        row_start, col_start, theta_block, beta_block, ratio = ratio_of(exp_theta, group, shard, position)
        part = jnp.dot(theta_block.T, ratio, preferred_element_type=jnp.float32)
        current = lax.dynamic_slice_in_dim(partial_value, col_start, TILE, 1)
        return lax.dynamic_update_slice_in_dim(partial_value, current + part, col_start, 1)

    def per_group(group, sstats):
        partial_value = over_shards(group, add_words, jnp.zeros(lambda_topics.shape, jnp.float32))
        rounded = lax.optimization_barrier(partial_value.astype(jnp.bfloat16))
        return sstats + rounded.astype(jnp.float32)

    sstats = lax.fori_loop(0, groups, per_group, jnp.zeros(lambda_topics.shape, jnp.float32))
    lambda_new = (1.0 - step_weight) * lambda_topics + step_weight * (eta_prior + corpus_scale * exp_beta.astype(jnp.float32) * sstats)
    return gamma, lambda_new
```

```python
import jax
import jax.numpy as jnp
from jax import lax
from jax.sharding import PartitionSpec as P

alpha_prior = 0.05
eta_prior = 0.01
step_weight = 0.5
corpus_scale = 4.0


def exp_digamma(x, offset):
    y = x + 4.0
    a = x * (x + 3.0)
    p = a * (a + 2.0)
    r = 1.0 / (p * y)
    q = p * r
    s = q * q
    shift = (2.0 * x + 3.0) * (2.0 * a + 2.0) * (y * r)
    tail = q * 0.5 + s * (1.0 / 12 - s * (1.0 / 120 - s * (1.0 / 252 - s * (1.0 / 240))))
    return y * jnp.exp(-(shift + tail) - offset)


def digamma(x):
    return jnp.log(exp_digamma(x, 0.0))


def expected_theta(gamma):
    return exp_digamma(gamma, digamma(jnp.sum(gamma, 1, keepdims=True))).astype(jnp.bfloat16)


def dense_counts(counts, place, rows, words):
    slots, tile, _ = counts.shape
    across = words // tile
    at = place[:, 0] * across + place[:, 1]
    slot_of = jnp.sum(jnp.where(at[:, None] == jnp.arange(slots)[None, :], jnp.arange(slots)[:, None], 0), 0)
    tiles = jnp.take(counts, slot_of, axis=0).astype(jnp.float32)
    return tiles.reshape(rows // tile, across, tile, tile).transpose(0, 2, 1, 3).reshape(rows, words)


def on_device(lambda_topics, gamma_start, tile_counts, tile_place, tile_live):
    rows, words = gamma_start.shape[0], lambda_topics.shape[1]
    counts = dense_counts(tile_counts[0, 0], tile_place[0, 0], rows, words)
    rowsum = lax.psum(jnp.sum(lambda_topics, 1), "vocab")
    share_beta = exp_digamma(lambda_topics, digamma(rowsum)[:, None]).astype(jnp.bfloat16)
    exp_beta = lax.all_gather(share_beta, "docs", axis=0, tiled=True)
    exp_theta = expected_theta(gamma_start)
    own_rows = rows // lax.axis_size("vocab")
    own_start = lax.axis_index("vocab") * own_rows

    def ratio_of(exp_theta):
        norm = jnp.dot(exp_theta, exp_beta, preferred_element_type=jnp.float32)
        return jnp.where(counts > 0, counts / norm, 0.0).astype(jnp.bfloat16)

    for step in range(3):
        part = lax.dot_general(
            ratio_of(exp_theta), exp_beta, (((1,), (1,)), ((), ())), preferred_element_type=jnp.float32
        )
        total = lax.psum_scatter(part.astype(jnp.bfloat16), "vocab", scatter_dimension=0, tiled=True)
        own_theta = lax.dynamic_slice_in_dim(exp_theta, own_start, own_rows, 0)
        gamma = alpha_prior + own_theta.astype(jnp.float32) * total.astype(jnp.float32)
        exp_theta = lax.all_gather(expected_theta(gamma), "vocab", axis=0, tiled=True)
    part_g = lax.dot_general(
        exp_theta, ratio_of(exp_theta), (((0,), (0,)), ((), ())), preferred_element_type=jnp.float32
    )
    sstats = lax.psum_scatter(part_g.astype(jnp.bfloat16), "docs", scatter_dimension=0, tiled=True)
    lambda_new = (1.0 - step_weight) * lambda_topics + step_weight * (
        eta_prior + corpus_scale * share_beta.astype(jnp.float32) * sstats.astype(jnp.float32)
    )
    return (gamma, lambda_new)


def solution(mesh):
    return jax.shard_map(
        on_device,
        mesh=mesh,
        in_specs=(
            P("docs", "vocab"),
            P(("parts", "docs"), None),
            P(("parts", "docs"), "vocab", None, None, None),
            P(("parts", "docs"), "vocab", None, None),
            P(("parts", "docs"), "vocab"),
        ),
        out_specs=(P(("parts", "docs", "vocab"), None), P(("parts", "docs"), "vocab")),
        check_vma=False,
    )
```

```python
import functools

import jax
import jax.numpy as jnp
from jax import lax
from jax.experimental import pallas as pl
from jax.experimental.pallas import tpu as pltpu
from jax.sharding import PartitionSpec as P

MESH = pl.DeviceIdType.MESH
ITERS = 3
UNIT = 32
TILE = 128
CHUNKS = 4
alpha_prior = 0.05
eta_prior = 0.01
step_weight = 0.5
corpus_scale = 4.0


def exp_digamma(x, offset):
    y = x + 4.0
    a = x * (x + 3.0)
    p = a * (a + 2.0)
    r = 1.0 / (p * y)
    q = p * r
    s = q * q
    shift = (2.0 * x + 3.0) * (2.0 * a + 2.0) * (y * r)
    tail = q * 0.5 + s * (1.0 / 12 - s * (1.0 / 120 - s * (1.0 / 252 - s * (1.0 / 240))))
    return y * jnp.exp(-(shift + tail) - offset)


def digamma(x):
    return jnp.log(exp_digamma(x, 0.0))


def remote(src, dst, send, recv, **where):
    return pltpu.make_async_remote_copy(
        src_ref=src, dst_ref=dst, send_sem=send, recv_sem=recv, device_id=where, device_id_type=MESH
    )


def kernel(
    nv, nd, place_ref, lam_ref, gamma_ref, counts_ref, gamma_out, lam_out,
    sums, shift, cd, beta, theta, part, ratio, from_left, from_right, to_right, to_left, gam, thall, rall, acc,
    sum_send, sum_recv, beta_send, beta_recv, rs, rr, ls, lr, th_send, th_recv, ra_send, ra_recv, fw_send,
):
    p, v, d = lax.axis_index("parts"), lax.axis_index("vocab"), lax.axis_index("docs")
    core = lax.rem(d, 2)
    sib = d + 1 - 2 * core
    share, words = lam_ref.shape
    rows, topics = gamma_ref.shape
    nb = 4
    block = rows // nb
    units = block // UNIT
    nx = nd // 2
    chip = lax.div(d, 2)
    others = [lax.rem(chip + i, nx) * 2 + core for i in range(1, nx)]
    peers = [lax.rem(d + i, nd) for i in range(1, nd)]

    barrier = pltpu.get_barrier_semaphore()
    for i in range(1, nv):
        pl.semaphore_signal(barrier, inc=1, device_id={"vocab": lax.rem(v + i, nv)}, device_id_type=MESH)
    for peer in peers:
        pl.semaphore_signal(barrier, inc=1, device_id={"docs": peer}, device_id_type=MESH)
    pl.semaphore_signal(barrier, inc=1, device_id={"parts": 1 - p}, device_id_type=MESH)

    folded = lam_ref[:, 0:TILE]
    for i in range(1, words // TILE):
        folded = folded + lam_ref[:, i * TILE : (i + 1) * TILE]
    sums[v] = jnp.broadcast_to(jnp.sum(folded.T, 0, keepdims=True), (8, share))
    pl.semaphore_wait(barrier, nv - 1 + nd - 1 + 1)

    def sum_copy(i):
        return remote(sums.at[v], sums.at[v], sum_send.at[i], sum_recv.at[v], vocab=lax.rem(v + i, nv))

    for i in range(1, nv):
        sum_copy(i).start()

    def first_theta(i, carry):
        at = pl.ds(pl.multiple_of(i * 16, 16), 16)
        g = gamma_ref[at, :]
        theta[at, :] = exp_digamma(g, digamma(jnp.sum(g, 1, keepdims=True))).astype(jnp.bfloat16)
        return carry

    lax.fori_loop(0, rows // 16, first_theta, 0)

    for i in range(1, nv):
        src = lax.rem(v + nv - i, nv)
        remote(sums.at[src], sums.at[src], sum_send.at[i], sum_recv.at[src], vocab=src).wait_recv()
    whole = sums[0]
    for i in range(1, nv):
        whole = whole + sums[i]
    shift[...] = jnp.broadcast_to(digamma(whole)[0:1], (TILE, share)).T

    piece = share // (2 * CHUNKS)

    def region(owner, c):
        return beta.at[pl.ds(pl.multiple_of(owner * share + c * piece, piece), piece)]

    def beta_copy(owner, c, slot, **where):
        return remote(region(owner, c), region(owner, c), beta_send.at[slot], beta_recv.at[owner, c], **where)

    sends = []

    def send_beta(owner, c, **where):
        copy = beta_copy(owner, c, len(sends), **where)
        copy.start()
        sends.append(copy)

    for j in range(2 * CHUNKS):
        c = lax.rem(p * CHUNKS + j, 2 * CHUNKS)

        def own_beta(i, carry, c=c):
            at = pl.ds(pl.multiple_of(c * piece + i * 16, 16), 16)
            to = pl.ds(pl.multiple_of(d * share + c * piece + i * 16, 16), 16)
            off = jnp.concatenate([shift[at, :]] * (words // TILE), 1)
            beta[to, :] = exp_digamma(lam_ref[at, :], off).astype(jnp.bfloat16)
            return carry

        lax.fori_loop(0, piece // 16, own_beta, 0)
        if j < CHUNKS:
            for other in others:
                send_beta(d, c, docs=other)
        send_beta(d, c, docs=sib)

    slots = counts_ref.shape[0]
    across = words // TILE
    for r in range(rows // TILE):
        for k in range(across):
            slot = jnp.int32(0)
            for s in range(slots):
                hit = place_ref[s, 0] * across + place_ref[s, 1] == r * across + k
                slot = jnp.where(hit, s, slot)
            cd[r * TILE : (r + 1) * TILE, k * TILE : (k + 1) * TILE] = counts_ref[slot].astype(jnp.float32)

    @pl.when(v == 0)
    def _():
        from_left[...] = jnp.zeros_like(from_left)

    @pl.when(v == nv - 1)
    def _():
        from_right[...] = jnp.zeros_like(from_right)

    for j in range(CHUNKS):
        c = p * CHUNKS + j
        for other in others:
            beta_copy(other, c, 0, docs=other).wait_recv()
            send_beta(other, c, parts=1 - p)
            send_beta(other, c, docs=sib)
    for j in range(CHUNKS):
        c = (1 - p) * CHUNKS + j
        for other in others:
            beta_copy(other, c, 0, docs=other).wait_recv()
            send_beta(other, c, docs=sib)
    for c in range(2 * CHUNKS):
        beta_copy(sib, c, 0, docs=sib).wait_recv()
        for other in others:
            far = other + 1 - 2 * core
            beta_copy(far, c, 0, docs=sib).wait_recv()

    def unit_rows(t, u):
        return pl.ds(pl.multiple_of(lax.rem(t, nb) * block + u * UNIT, UNIT), UNIT)

    def right_copy(t, u):
        it, at, n = lax.div(t, nb), unit_rows(t, u), lax.rem(t, nb) * units + u
        return remote(to_right.at[it, at], from_left.at[it, at], rs.at[it, n], rr.at[it, n], vocab=lax.rem(v + 1, nv))

    def left_copy(t, u):
        it, at, n = lax.div(t, nb), unit_rows(t, u), lax.rem(t, nb) * units + u
        return remote(
            to_left.at[it, at], from_right.at[it, at], ls.at[it, n], lr.at[it, n], vocab=lax.rem(v + nv - 1, nv)
        )

    total_steps = ITERS * nb

    def pass_right(t):
        for u in range(units):
            it, at = lax.div(t, nb), unit_rows(t, u)

            @pl.when(v > 0)
            def _():
                right_copy(t, u).wait_recv()

            to_right[it, at, :] = (part[at, :] + from_left[it, at, :].astype(jnp.float32)).astype(jnp.bfloat16)
            right_copy(t, u).start()

    def pass_left(t):
        for u in range(units):
            it, at = lax.div(t, nb), unit_rows(t, u)

            @pl.when(v < nv - 1)
            def _():
                left_copy(t, u).wait_recv()

            to_left[it, at, :] = (part[at, :] + from_right[it, at, :].astype(jnp.float32)).astype(jnp.bfloat16)
            left_copy(t, u).start()

    def finish(t):
        it = lax.div(t, nb)
        for u in range(units):

            @pl.when(v == nv - 1)
            def _():
                right_copy(t, u).wait_recv()

            @pl.when(v == 0)
            def _():
                left_copy(t, u).wait_recv()

            def some(i, carry):
                at = pl.ds(pl.multiple_of(lax.rem(t, nb) * block + u * UNIT + i * 16, 16), 16)
                total = part[at, :] + (
                    from_left[it, at, :].astype(jnp.float32) + from_right[it, at, :].astype(jnp.float32)
                )
                g = alpha_prior + theta[at, :].astype(jnp.float32) * total
                gam[at, :] = g
                theta[at, :] = exp_digamma(g, digamma(jnp.sum(g, 1, keepdims=True))).astype(jnp.bfloat16)
                return carry

            lax.fori_loop(0, UNIT // 16, some, 0)

    def th_copy(b, to):
        at = pl.ds(pl.multiple_of(b * block, block), block)
        cols = pl.ds(pl.multiple_of(to * share, share), share)
        return remote(theta.at[at, cols], thall.at[b, d], th_send.at[b, to], th_recv.at[b, d], docs=to)

    def ra_copy(b, to):
        at = pl.ds(pl.multiple_of(b * block, block), block)
        return remote(ratio.at[at], rall.at[b, d], ra_send.at[b, to], ra_recv.at[b, d], docs=to)

    def fw_copy(b, owner):
        return remote(rall.at[b, owner], rall.at[b, owner], fw_send.at[b, owner], ra_recv.at[b, owner], docs=sib)

    def th_from(b, owner):
        return remote(thall.at[b, owner], thall.at[b, owner], th_send.at[b, owner], th_recv.at[b, owner], docs=sib)

    wide = 256

    def compute(s):
        b = lax.rem(s, nb)
        at = pl.ds(pl.multiple_of(b * block, block), block)
        th = theta[at, :]
        for k in range(words // wide):
            cols = slice(k * wide, (k + 1) * wide)
            norm = jnp.dot(th, beta[:, cols], preferred_element_type=jnp.float32)
            c = cd[at, cols]
            ratio[at, cols] = jnp.where(c > 0.0, c / norm, 0.0).astype(jnp.bfloat16)

        @pl.when(s < total_steps)
        def _():
            ra = ratio[at, :]
            for k in range(topics // wide):
                cols = slice(k * wide, (k + 1) * wide)
                part[at, cols] = lax.dot_general(
                    ra, beta[cols, :], (((1,), (1,)), ((), ())), preferred_element_type=jnp.float32
                )

        @pl.when(s >= total_steps)
        def _():
            for other in others:
                ra_copy(b, other).start()
            for to in peers:
                th_copy(b, to).start()
            ra_copy(b, sib).start()
            thall[b, d] = theta[at, pl.ds(pl.multiple_of(d * share, share), share)]
            rall[b, d] = ratio[at, :]

    def forward(b):
        for other in others:
            fw_copy(b, other).wait_recv()
            fw_copy(b, other).start()

    def collect(b):
        for peer in peers:
            th_from(b, peer).wait_recv()
        fw_copy(b, sib).wait_recv()
        for other in others:
            fw_copy(b, other + 1 - 2 * core).wait_recv()
        left = thall[b].reshape(nd * block, share)
        for k in range(words // wide):
            cols = slice(k * wide, (k + 1) * wide)
            right = rall[b, :, :, cols].reshape(nd * block, wide)
            more = lax.dot_general(left, right, (((0,), (0,)), ((), ())), preferred_element_type=jnp.float32)
            acc[:, cols] = acc[:, cols] + more

    acc[...] = jnp.zeros_like(acc)
    lag_right = jnp.minimum(v, 2)
    lag_left = jnp.minimum(nv - 1 - v, 2)

    def step(s, carry):
        t_right = s - lag_right

        @pl.when((v > 0) & (v < nv - 1) & (t_right >= 0) & (t_right < total_steps))
        def _():
            pass_right(t_right)

        t_left = s - lag_left

        @pl.when((v > 0) & (v < nv - 1) & (t_left >= 0) & (t_left < total_steps))
        def _():
            pass_left(t_left)

        @pl.when(s < total_steps + nb)
        def _():
            compute(s)

        @pl.when((v == 0) & (s < total_steps))
        def _():
            pass_right(s)

        @pl.when((v == nv - 1) & (s < total_steps))
        def _():
            pass_left(s)

        @pl.when((s >= 3) & (s < total_steps + 3))
        def _():
            finish(s - 3)

        @pl.when(s > total_steps)
        def _():
            @pl.when(s <= total_steps + nb)
            def _():
                forward(s - total_steps - 1)

            @pl.when(s > total_steps + 1)
            def _():
                collect(s - total_steps - 2)

        return carry

    lax.fori_loop(0, total_steps + nb + 2, step, 0)

    own = gamma_out.shape[0]
    gamma_out[...] = gam[pl.ds(pl.multiple_of(v * own, own), own), :]

    def update(i, carry):
        at = pl.ds(pl.multiple_of(i * 16, 16), 16)
        mine = beta[pl.ds(pl.multiple_of(d * share + i * 16, 16), 16), :].astype(jnp.float32)
        lam_out[at, :] = (1.0 - step_weight) * lam_ref[at, :] + step_weight * (
            eta_prior + corpus_scale * mine * acc[at, :]
        )
        return carry

    lax.fori_loop(0, share // 16, update, 0)

    for i in range(1, nv):
        sum_copy(i).wait_send()
    for copy in sends:
        copy.wait_send()

    def drain(t, carry):
        for u in range(units):

            @pl.when(v < nv - 1)
            def _():
                right_copy(t, u).wait_send()

            @pl.when(v > 0)
            def _():
                left_copy(t, u).wait_send()

        return carry

    lax.fori_loop(0, total_steps, drain, 0)

    def drain_last(b, carry):
        for other in others:
            ra_copy(b, other).wait_send()
            fw_copy(b, other).wait_send()
        ra_copy(b, sib).wait_send()
        for to in peers:
            th_copy(b, to).wait_send()
        return carry

    lax.fori_loop(0, nb, drain_last, 0)


def on_device(nv, nd, lambda_topics, gamma_start, tile_counts, tile_place, tile_live):
    share, words = lambda_topics.shape
    rows, topics = gamma_start.shape
    nb, nx = 4, nd // 2
    nsend = CHUNKS * (2 + (nx - 1) * 4)
    vmem = pl.BlockSpec(memory_space=pltpu.VMEM)
    bf, f32 = jnp.bfloat16, jnp.float32
    dma = pltpu.SemaphoreType.DMA
    units = rows // UNIT
    moving = pltpu.VMEM((ITERS, rows, topics), bf)
    return pl.pallas_call(
        functools.partial(kernel, nv, nd),
        out_shape=(
            jax.ShapeDtypeStruct((rows // nv, topics), f32),
            jax.ShapeDtypeStruct((share, words), f32),
        ),
        in_specs=[pl.BlockSpec(memory_space=pltpu.SMEM), vmem, vmem, vmem],
        out_specs=(vmem, vmem),
        scratch_shapes=[
            pltpu.VMEM((nv, 8, share), f32),
            pltpu.VMEM((share, TILE), f32),
            pltpu.VMEM((rows, words), f32),
            pltpu.VMEM((topics, words), bf),
            pltpu.VMEM((rows, topics), bf),
            pltpu.VMEM((rows, topics), f32),
            pltpu.VMEM((rows, words), bf),
            moving, moving, moving, moving,
            pltpu.VMEM((rows, topics), f32),
            pltpu.VMEM((nb, nd, rows // nb, share), bf),
            pltpu.VMEM((nb, nd, rows // nb, words), bf),
            pltpu.VMEM((share, words), f32),
            dma((nv,)), dma((nv,)),
            dma((nsend,)), dma((nd, 2 * CHUNKS)),
            dma((ITERS, units)), dma((ITERS, units)), dma((ITERS, units)), dma((ITERS, units)),
            dma((nb, nd)), dma((nb, nd)), dma((nb, nd)), dma((nb, nd)), dma((nb, nd)),
        ],
        compiler_params=pltpu.CompilerParams(
            collective_id=0, has_side_effects=True, vmem_limit_bytes=56 * 1024 * 1024
        ),
    )(tile_place[0, 0], lambda_topics, gamma_start, tile_counts[0, 0])


def solution(mesh):
    return jax.shard_map(
        functools.partial(on_device, mesh.shape["vocab"], mesh.shape["docs"]),
        mesh=mesh,
        in_specs=(
            P("docs", "vocab"),
            P(("parts", "docs"), None),
            P(("parts", "docs"), "vocab", None, None, None),
            P(("parts", "docs"), "vocab", None, None),
            P(("parts", "docs"), "vocab"),
        ),
        out_specs=(P(("parts", "docs", "vocab"), None), P(("parts", "docs"), "vocab")),
        check_vma=False,
    )
```

```python
import functools

import jax
import jax.numpy as jnp
from jax import lax
from jax.experimental import pallas as pl
from jax.experimental.pallas import tpu as pltpu
from jax.sharding import PartitionSpec as P

MESH = pl.DeviceIdType.MESH
ITERS = 3
UNIT = 16
TILE = 128
CHUNKS = 8
alpha_prior = 0.05
eta_prior = 0.01
step_weight = 0.5
corpus_scale = 4.0


def exp_digamma(x, offset):
    y = x + 4.0
    a = x * (x + 3.0)
    p = a * (a + 2.0)
    r = 1.0 / (p * y)
    q = p * r
    s = q * q
    shift = (2.0 * x + 3.0) * (2.0 * a + 2.0) * (y * r)
    tail = q * 0.5 + s * (1.0 / 12 - s * (1.0 / 120 - s * (1.0 / 252 - s * (1.0 / 240))))
    return y * jnp.exp(-(shift + tail) - offset)


def digamma(x):
    return jnp.log(exp_digamma(x, 0.0))


def remote(src, dst, send, recv, **where):
    return pltpu.make_async_remote_copy(
        src_ref=src, dst_ref=dst, send_sem=send, recv_sem=recv, device_id=where, device_id_type=MESH
    )


def kernel(
    nv, nd, place_ref, lam_hbm, gamma_hbm, counts_hbm, gamma_out, lam_out,
    lam_ref, gamma_ref, counts_ref, lam_new, load_sem, store_sem, sums, offs, off, psums, cd, beta, theta, part, ratio, from_left, from_right, to_right, to_left, gam, thall, rall, acc,
    sum_send, sum_recv, off_send, off_recv, beta_send, beta_recv, rs, rr, ls, lr, th_send, th_recv, ra_send, ra_recv, fw_send,
):
    p, v, d = lax.axis_index("parts"), lax.axis_index("vocab"), lax.axis_index("docs")
    load_lam = pltpu.make_async_copy(lam_hbm, lam_ref, load_sem.at[0])
    load_gamma = pltpu.make_async_copy(gamma_hbm, gamma_ref, load_sem.at[1])
    load_counts = pltpu.make_async_copy(counts_hbm, counts_ref, load_sem.at[2])
    load_lam.start()
    load_counts.start()
    load_gamma.start()
    core = lax.rem(d, 2)
    sib = d + 1 - 2 * core
    share, words = lam_ref.shape
    rows, topics = gamma_ref.shape
    nb = 4
    block = rows // nb
    units = block // UNIT
    nx = nd // 2
    chip = lax.div(d, 2)
    others = [lax.rem(chip + i, nx) * 2 + core for i in range(1, nx)]
    peers = [lax.rem(d + i, nd) for i in range(1, nd)]

    barrier = pltpu.get_barrier_semaphore()
    for i in range(1, nv):
        pl.semaphore_signal(barrier, inc=1, device_id={"vocab": lax.rem(v + i, nv)}, device_id_type=MESH)
    for peer in peers:
        pl.semaphore_signal(barrier, inc=1, device_id={"docs": peer}, device_id_type=MESH)
    pl.semaphore_signal(barrier, inc=1, device_id={"parts": 1 - p}, device_id_type=MESH)

    piece = share // (2 * CHUNKS)

    def region(owner, c):
        return beta.at[pl.ds(pl.multiple_of(owner * share + c * piece, piece), piece)]

    def beta_copy(owner, c, slot, **where):
        return remote(region(owner, c), region(owner, c), beta_send.at[slot], beta_recv.at[owner, c], **where)

    sends = []

    def send_beta(owner, c, **where):
        copy = beta_copy(owner, c, len(sends), **where)
        copy.start()
        sends.append(copy)

    load_lam.wait()
    for j in range(2 * CHUNKS):
        c = lax.rem(p * CHUNKS + j, 2 * CHUNKS)
        for i in range(piece // 16):
            at = pl.ds(pl.multiple_of(c * piece + i * 16, 16), 16)
            to = pl.ds(pl.multiple_of(d * share + c * piece + i * 16, 16), 16)
            beta[to, :] = exp_digamma(lam_ref[at, :], 0.0).astype(jnp.bfloat16)
        if j == 0:
            pl.semaphore_wait(barrier, nv - 1 + nd - 1 + 1)
        if j < CHUNKS:
            for other in others:
                send_beta(d, c, docs=other)
        send_beta(d, c, docs=sib)

    folded = lam_ref[:, 0:TILE]
    for i in range(1, words // TILE):
        folded = folded + lam_ref[:, i * TILE : (i + 1) * TILE]
    sums[v] = jnp.broadcast_to(jnp.sum(folded.T, 0, keepdims=True), (8, share))

    def sum_copy(i):
        return remote(sums.at[v], sums.at[v], sum_send.at[i], sum_recv.at[v], vocab=lax.rem(v + i, nv))

    for i in range(1, nv):
        sum_copy(i).start()

    slots = counts_ref.shape[0]
    across = words // TILE
    load_counts.wait()
    for r in range(rows // TILE):
        for k in range(across):
            slot = jnp.int32(0)
            for s in range(slots):
                hit = place_ref[0, s] * across + place_ref[1, s] == r * across + k
                slot = jnp.where(hit, s, slot)
            cd[r * TILE : (r + 1) * TILE, k * TILE : (k + 1) * TILE] = counts_ref[slot].astype(jnp.float32)

    @pl.when(v == 0)
    def _():
        from_left[...] = jnp.zeros_like(from_left)

    @pl.when(v == nv - 1)
    def _():
        from_right[...] = jnp.zeros_like(from_right)

    acc[...] = jnp.zeros_like(acc)

    def off_copy(i):
        return remote(offs.at[d], offs.at[d], off_send.at[i], off_recv.at[d], docs=lax.rem(d + i, nd))

    def send_offs():
        for i in range(1, nv):
            src = lax.rem(v + nv - i, nv)
            remote(sums.at[src], sums.at[src], sum_send.at[i], sum_recv.at[src], vocab=src).wait_recv()
        whole = sums[0]
        for i in range(1, nv):
            whole = whole + sums[i]
        offs[d] = digamma(whole)
        for i in range(1, nd):
            off_copy(i).start()

    def take_offs():
        for i in range(1, nd):
            src = lax.rem(d + nd - i, nd)
            remote(offs.at[src], offs.at[src], off_send.at[i], off_recv.at[src], docs=src).wait_recv()
        for i in range(nd):
            off[:, i * share : (i + 1) * share] = offs[i]
        load_gamma.wait()

    def set_theta(at, n):
        for i in range(n // 16):
            part_of = pl.ds(pl.multiple_of(at + i * 16, 16), 16)
            psums[i * 16 : (i + 1) * 16, :] = jnp.broadcast_to(jnp.sum(gam[part_of, :], 1, keepdims=True), (16, TILE))
        psums[0:n, :] = digamma(psums[0:n, :])
        for i in range(n // 16):
            part_of = pl.ds(pl.multiple_of(at + i * 16, 16), 16)
            offset = psums[i * 16 : (i + 1) * 16, 0:1] + off[0:1, :]
            theta[part_of, :] = exp_digamma(gam[part_of, :], offset).astype(jnp.bfloat16)

    first = rows // 8

    def first_theta(i):
        at = pl.ds(i * first, first)
        gam[at, :] = gamma_ref[at, :]
        set_theta(i * first, first)

    for j in range(CHUNKS):
        c = p * CHUNKS + j
        for other in others:
            beta_copy(other, c, 0, docs=other).wait_recv()
            send_beta(other, c, parts=1 - p)
            send_beta(other, c, docs=sib)
        if j == 1:
            send_offs()
        if j == CHUNKS - 3:
            take_offs()
        if j >= CHUNKS - 3:
            first_theta(j - CHUNKS + 3)
    for j in range(CHUNKS):
        c = (1 - p) * CHUNKS + j
        for other in others:
            beta_copy(other, c, 0, docs=other).wait_recv()
            send_beta(other, c, docs=sib)
        if j % 2 == 0:
            first_theta(3 + j // 2)
    first_theta(7)
    for c in range(2 * CHUNKS):
        beta_copy(sib, c, 0, docs=sib).wait_recv()
        for other in others:
            far = other + 1 - 2 * core
            beta_copy(far, c, 0, docs=sib).wait_recv()

    def unit_rows(t, u):
        return pl.ds(pl.multiple_of(lax.rem(t, nb) * block + u * UNIT, UNIT), UNIT)

    def right_copy(t, u):
        it, at, n = lax.div(t, nb), unit_rows(t, u), lax.rem(t, nb) * units + u
        return remote(to_right.at[it, at], from_left.at[it, at], rs.at[it, n], rr.at[it, n], vocab=lax.rem(v + 1, nv))

    def left_copy(t, u):
        it, at, n = lax.div(t, nb), unit_rows(t, u), lax.rem(t, nb) * units + u
        return remote(
            to_left.at[it, at], from_right.at[it, at], ls.at[it, n], lr.at[it, n], vocab=lax.rem(v + nv - 1, nv)
        )

    total_steps = ITERS * nb

    def pass_right(t):
        for u in range(units):
            it, at = lax.div(t, nb), unit_rows(t, u)

            @pl.when(v > 0)
            def _():
                right_copy(t, u).wait_recv()

            to_right[it, at, :] = (part[at, :] + from_left[it, at, :].astype(jnp.float32)).astype(jnp.bfloat16)
            right_copy(t, u).start()

    def pass_left(t):
        for u in range(units):
            it, at = lax.div(t, nb), unit_rows(t, u)

            @pl.when(v < nv - 1)
            def _():
                left_copy(t, u).wait_recv()

            to_left[it, at, :] = (part[at, :] + from_right[it, at, :].astype(jnp.float32)).astype(jnp.bfloat16)
            left_copy(t, u).start()

    def finish(t):
        it = lax.div(t, nb)
        for u in range(units):

            @pl.when(v == nv - 1)
            def _():
                right_copy(t, u).wait_recv()

            @pl.when(v == 0)
            def _():
                left_copy(t, u).wait_recv()

            at = unit_rows(t, u)
            total = part[at, :] + (
                from_left[it, at, :].astype(jnp.float32) + from_right[it, at, :].astype(jnp.float32)
            )
            gam[at, :] = alpha_prior + theta[at, :].astype(jnp.float32) * total
        set_theta(lax.rem(t, nb) * block, block)

        @pl.when(t >= total_steps - nb)
        def _():
            for to in peers:
                th_copy(lax.rem(t, nb), to).start()

    def th_copy(b, to):
        at = pl.ds(pl.multiple_of(b * block, block), block)
        cols = pl.ds(pl.multiple_of(to * share, share), share)
        return remote(theta.at[at, cols], thall.at[b, d], th_send.at[b, to], th_recv.at[b, d], docs=to)

    def ra_copy(b, to):
        at = pl.ds(pl.multiple_of(b * block, block), block)
        return remote(ratio.at[at], rall.at[b, d], ra_send.at[b, to], ra_recv.at[b, d], docs=to)

    def fw_copy(b, owner):
        return remote(rall.at[b, owner], rall.at[b, owner], fw_send.at[b, owner], ra_recv.at[b, owner], docs=sib)

    def th_from(b, owner):
        return remote(thall.at[b, owner], thall.at[b, owner], th_send.at[b, owner], th_recv.at[b, owner], docs=sib)

    wide = 256

    def compute(s):
        b = lax.rem(s, nb)
        at = pl.ds(pl.multiple_of(b * block, block), block)
        th = theta[at, :]
        for k in range(words // wide):
            cols = slice(k * wide, (k + 1) * wide)
            norm = jnp.dot(th, beta[:, cols], preferred_element_type=jnp.float32)
            c = cd[at, cols]
            ratio[at, cols] = jnp.where(c > 0.0, c / norm, 0.0).astype(jnp.bfloat16)

        @pl.when(s < total_steps)
        def _():
            ra = ratio[at, :]
            for k in range(topics // wide):
                cols = slice(k * wide, (k + 1) * wide)
                part[at, cols] = lax.dot_general(
                    ra, beta[cols, :], (((1,), (1,)), ((), ())), preferred_element_type=jnp.float32
                )

        @pl.when(s >= total_steps)
        def _():
            for other in others:
                ra_copy(b, other).start()
            ra_copy(b, sib).start()
            thall[b, d] = theta[at, pl.ds(pl.multiple_of(d * share, share), share)]
            rall[b, d] = ratio[at, :]

    def forward(b):
        for other in others:
            fw_copy(b, other).wait_recv()
            fw_copy(b, other).start()

    def collect(b):
        for peer in peers:
            th_from(b, peer).wait_recv()
        fw_copy(b, sib).wait_recv()
        for other in others:
            fw_copy(b, other + 1 - 2 * core).wait_recv()
        left = thall[b].reshape(nd * block, share)
        for k in range(words // wide):
            cols = slice(k * wide, (k + 1) * wide)
            right = rall[b, :, :, cols].reshape(nd * block, wide)
            more = lax.dot_general(left, right, (((0,), (0,)), ((), ())), preferred_element_type=jnp.float32)
            acc[:, cols] = acc[:, cols] + more

    lag_right = jnp.minimum(v, 2)
    lag_left = jnp.minimum(nv - 1 - v, 2)

    own = gamma_out.shape[0]
    own_at = pl.ds(pl.multiple_of(v * own, own), own)
    store_gamma = pltpu.make_async_copy(gam.at[own_at], gamma_out, store_sem.at[0])

    def step(s, carry):
        t_right = s - lag_right

        @pl.when((v > 0) & (v < nv - 1) & (t_right >= 0) & (t_right < total_steps))
        def _():
            pass_right(t_right)

        t_left = s - lag_left

        @pl.when((v > 0) & (v < nv - 1) & (t_left >= 0) & (t_left < total_steps))
        def _():
            pass_left(t_left)

        @pl.when(s < total_steps + nb)
        def _():
            compute(s)

        @pl.when((v == 0) & (s < total_steps))
        def _():
            pass_right(s)

        @pl.when((v == nv - 1) & (s < total_steps))
        def _():
            pass_left(s)

        @pl.when((s >= 3) & (s < total_steps + 3))
        def _():
            finish(s - 3)

        @pl.when(s == total_steps + 3)
        def _():
            store_gamma.start()

        @pl.when(s > total_steps)
        def _():
            @pl.when(s <= total_steps + nb)
            def _():
                forward(s - total_steps - 1)

            @pl.when(s > total_steps + 1)
            def _():
                collect(s - total_steps - 2)

        return carry

    lax.fori_loop(0, total_steps + nb + 2, step, 0)

    big = share // 4
    stores = []
    for k in range(4):

        def update(i, carry, k=k):
            at = pl.ds(pl.multiple_of(k * big + i * 16, 16), 16)
            mine = beta[pl.ds(pl.multiple_of(d * share + k * big + i * 16, 16), 16), :].astype(jnp.float32)
            lam_new[at, :] = (1.0 - step_weight) * lam_ref[at, :] + step_weight * (
                eta_prior + corpus_scale * mine * acc[at, :]
            )
            return carry

        lax.fori_loop(0, big // 16, update, 0)
        at = pl.ds(k * big, big)
        store = pltpu.make_async_copy(lam_new.at[at], lam_out.at[at], store_sem.at[1 + k])
        store.start()
        stores.append(store)

    for i in range(1, nd):
        off_copy(i).wait_send()
    for i in range(1, nv):
        sum_copy(i).wait_send()
    for copy in sends:
        copy.wait_send()

    def drain(t, carry):
        for u in range(units):

            @pl.when(v < nv - 1)
            def _():
                right_copy(t, u).wait_send()

            @pl.when(v > 0)
            def _():
                left_copy(t, u).wait_send()

        return carry

    lax.fori_loop(0, total_steps, drain, 0)

    def drain_last(b, carry):
        for other in others:
            ra_copy(b, other).wait_send()
            fw_copy(b, other).wait_send()
        ra_copy(b, sib).wait_send()
        for to in peers:
            th_copy(b, to).wait_send()
        return carry

    lax.fori_loop(0, nb, drain_last, 0)
    for store in stores:
        store.wait()
    store_gamma.wait()


def on_device(nv, nd, lambda_topics, gamma_start, tile_counts, tile_place, tile_live):
    share, words = lambda_topics.shape
    rows, topics = gamma_start.shape
    nb, nx = 4, nd // 2
    nsend = CHUNKS * (2 + (nx - 1) * 4)
    hbm = pl.BlockSpec(memory_space=pl.ANY)
    bf, f32 = jnp.bfloat16, jnp.float32
    dma = pltpu.SemaphoreType.DMA
    units = rows // UNIT
    moving = pltpu.VMEM((ITERS, rows, topics), bf)
    return pl.pallas_call(
        functools.partial(kernel, nv, nd),
        out_shape=(
            jax.ShapeDtypeStruct((rows // nv, topics), f32),
            jax.ShapeDtypeStruct((share, words), f32),
        ),
        in_specs=[pl.BlockSpec(memory_space=pltpu.SMEM), hbm, hbm, hbm],
        out_specs=(hbm, hbm),
        scratch_shapes=[
            pltpu.VMEM((share, words), f32),
            pltpu.VMEM((rows, topics), f32),
            pltpu.VMEM(tile_counts.shape[2:], jnp.int32),
            pltpu.VMEM((share, words), f32),
            dma((3,)), dma((5,)),
            pltpu.VMEM((nv, 8, share), f32),
            pltpu.VMEM((nd, 8, share), f32),
            pltpu.VMEM((8, topics), f32),
            pltpu.VMEM((rows // nb, TILE), f32),
            pltpu.VMEM((rows, words), f32),
            pltpu.VMEM((topics, words), bf),
            pltpu.VMEM((rows, topics), bf),
            pltpu.VMEM((rows, topics), f32),
            pltpu.VMEM((rows, words), bf),
            moving, moving, moving, moving,
            pltpu.VMEM((rows, topics), f32),
            pltpu.VMEM((nb, nd, rows // nb, share), bf),
            pltpu.VMEM((nb, nd, rows // nb, words), bf),
            pltpu.VMEM((share, words), f32),
            dma((nv,)), dma((nv,)), dma((nd,)), dma((nd,)),
            dma((nsend,)), dma((nd, 2 * CHUNKS)),
            dma((ITERS, units)), dma((ITERS, units)), dma((ITERS, units)), dma((ITERS, units)),
            dma((nb, nd)), dma((nb, nd)), dma((nb, nd)), dma((nb, nd)), dma((nb, nd)),
        ],
        compiler_params=pltpu.CompilerParams(
            collective_id=0, has_side_effects=True, vmem_limit_bytes=56 * 1024 * 1024
        ),
    )(tile_place[0, 0].T, lambda_topics, gamma_start, tile_counts[0, 0])


def solution(mesh):
    return jax.shard_map(
        functools.partial(on_device, mesh.shape["vocab"], mesh.shape["docs"]),
        mesh=mesh,
        in_specs=(
            P("docs", "vocab"),
            P(("parts", "docs"), None),
            P(("parts", "docs"), "vocab", None, None, None),
            P(("parts", "docs"), "vocab", None, None),
            P(("parts", "docs"), "vocab"),
        ),
        out_specs=(P(("parts", "docs", "vocab"), None), P(("parts", "docs"), "vocab")),
        check_vma=False,
    )
```
